32 devices in a mesh: seq: 2 (over x), fsdp: 16 (over z, y, core).
Axes of the slice: x: 2, y: 2, z: 4, core: 2. Of those that a mesh axis runs over, the one named last changes fastest.
Arguments:
- block_input: float32 [16, 512, 1024], P('fsdp', 'seq'), may hold values from -6 to 6
- key_mask: int32 [16, 512], P('fsdp'), may hold values from 0 to 1, as said below
- first_gain: bfloat16 [1024], P('fsdp'), may hold values from 0.5 to 1.5
- first_shift: bfloat16 [1024], P('fsdp'), may hold values from -3 to 3
- qkv_weight: bfloat16 [1024, 3072], P('fsdp'), may hold values from -0.1875 to 0.1875
- query_bias: bfloat16 [1024], P('fsdp'), may hold values from -3 to 3
- value_bias: bfloat16 [1024], P('fsdp'), may hold values from -3 to 3
- proj_weight: bfloat16 [1024, 1024], P('fsdp'), may hold values from -1.5 to 1.5
- proj_bias: bfloat16 [1024], P('fsdp'), may hold values from -3 to 3
- first_scale: bfloat16 [1024], P('fsdp'), may hold values from 0.5 to 2
- second_gain: bfloat16 [1024], P('fsdp'), may hold values from 0.5 to 1.5
- second_shift: bfloat16 [1024], P('fsdp'), may hold values from -3 to 3
- fc1_weight: bfloat16 [1024, 4096], P('fsdp'), may hold values from -0.1875 to 0.1875
- fc1_bias: bfloat16 [4096], P('fsdp'), may hold values from -3 to 3
- fc2_weight: bfloat16 [4096, 1024], P('fsdp'), may hold values from -0.09375 to 0.09375
- fc2_bias: bfloat16 [1024], P('fsdp'), may hold values from -3 to 3
- second_scale: bfloat16 [1024], P('fsdp'), may hold values from 0.5 to 2
- cotangent: float32 [16, 512, 1024], P('fsdp', 'seq'), may hold values from -6 to 6
Outputs:
- block_output: float32 [16, 512, 1024], P('fsdp', 'seq')
- input_grad: float32 [16, 512, 1024], P('fsdp', 'seq')
- first_gain_grad: float32 [1024], P('fsdp')
- first_shift_grad: float32 [1024], P('fsdp')
- qkv_weight_grad: float32 [1024, 3072], P('fsdp')
- query_bias_grad: float32 [1024], P('fsdp')
- value_bias_grad: float32 [1024], P('fsdp')
- proj_weight_grad: float32 [1024, 1024], P('fsdp')
- proj_bias_grad: float32 [1024], P('fsdp')
- first_scale_grad: float32 [1024], P('fsdp')
- second_gain_grad: float32 [1024], P('fsdp')
- second_shift_grad: float32 [1024], P('fsdp')
- fc1_weight_grad: float32 [1024, 4096], P('fsdp')
- fc1_bias_grad: float32 [4096], P('fsdp')
- fc2_weight_grad: float32 [4096, 1024], P('fsdp')
- fc2_bias_grad: float32 [1024], P('fsdp')
- second_scale_grad: float32 [1024], P('fsdp')
The draws below stay inside these ranges and needn't reach their ends.
Inputs may be any that keep to these rules, and one draw needn't show every extreme that they name: `key_mask`: each row is ones on a leading run of positions and zeros after it; its first position is 1 and its last is 0.
All inputs are finite; a program needn't handle non-finite values.
Results may differ from the reference program's by a relative error of at most 0.012.
The reference program's roundings to bfloat16 on the way count: a program that leaves them out, or rounds other values in their place, can miss the bound.
Values may be sent and summed in bfloat16 or wider, within the bound.
A program may use at most 192 MiB of HBM per device.

```python
import math
import jax
import jax.numpy as jnp
from jax import lax

D = 1024
HEADS = 16
HD = 64
FF = 4096
LEN = 512
IMAGES = 16


def draw_key_mask(key, part):
    lengths = LEN - 1 - jax.random.randint(jax.random.fold_in(key, 5), (IMAGES, 1), 0, LEN // 2)
    positions = jnp.arange(LEN, dtype=jnp.int32)[None, :]
    return (positions < lengths).astype(jnp.int32)


def strengthened(values, key, source, target, parts, factor):
    def block_of(position):
        return (jnp.arange(values.shape[position]) // (values.shape[position] // parts)).reshape((-1,) + (1,) * (values.ndim - 1 - position))

    one_side = jax.random.permutation(key, parts)[block_of(target)]
    far = (block_of(target) + parts // 2) % parts
    return jnp.where((block_of(source) == one_side) | (block_of(source) == far), factor * values, values)


def level_of(key, extent, cuts, smallest, largest):
    level, own = 1.0, jax.random.fold_in(key, 6)
    for axis_at, parts in cuts:
        steps = jnp.exp(jax.random.uniform(jax.random.fold_in(own, axis_at), (parts,), jnp.float32, smallest / len(cuts), largest / len(cuts)))
        level = level * jnp.repeat(steps, extent[axis_at] // parts).reshape([-1 if axis == axis_at else 1 for axis in range(len(extent))])
    return level


def scatter_about(own_key, shape, scale, reach, pieces=(), kind=jnp.bfloat16):
    values = jax.random.normal(own_key, shape, jnp.float32) * scale
    if len(pieces) > 0:
        values = level_of(own_key, shape, pieces, -0.22, 0.18) * values
    return jnp.clip(values, min=-reach, max=reach).astype(kind)


def bell_draw_with(own_key, extent, width, bound, split, heavy, kind=jnp.bfloat16):
    array = width * jax.random.normal(own_key, extent, jnp.float32)
    if split:
        array = array * level_of(own_key, extent, split, -0.22, 0.18)
    return jnp.clip(strengthened(array, jax.random.fold_in(own_key, 3), *heavy), -bound, bound).astype(kind)


def setup_inputs(seed: int = 0) -> dict:
    seeds = jax.random.split(jax.random.key(seed), 19)
    return {
        "block_input": scatter_about(seeds[0], (IMAGES, LEN, D), 1.0, 6.0, ((0, 16), (1, 2)), jnp.float32),
        "key_mask": draw_key_mask(jax.random.fold_in(seeds[18], 71), 0),
        "first_gain": jnp.clip(1.0 + 0.1 * jax.random.normal(seeds[2], (D,), jnp.float32), 0.5, 1.5).astype(jnp.bfloat16),
        "first_shift": scatter_about(seeds[3], (D,), 0.5, 3.0, ((0, 16),)),
        "qkv_weight": scatter_about(seeds[4], (D, 3 * D), D ** -0.5, 0.1875, ((0, 16),)),
        "query_bias": scatter_about(seeds[5], (D,), 0.5, 3.0, ((0, 16),)),
        "value_bias": scatter_about(seeds[6], (D,), 0.5, 3.0, ((0, 16),)),
        "proj_weight": scatter_about(seeds[7], (D, D), (D // 64) ** -0.5, 1.5, ((0, 16),)),
        "proj_bias": scatter_about(seeds[8], (D,), 0.5, 3.0, ((0, 16),)),
        "first_scale": jnp.clip(jnp.exp(math.log(2.0) - 1.3862944 * jax.random.uniform(seeds[9], (D,), jnp.float32) ** level_of(seeds[9], (D,), ((0, 16),), -0.2, 0.2)), 0.5, 2.0).astype(jnp.bfloat16),
        "second_gain": jnp.clip(1.0 + 0.1 * jax.random.normal(seeds[10], (D,), jnp.float32), 0.5, 1.5).astype(jnp.bfloat16),
        "second_shift": scatter_about(seeds[11], (D,), 0.5, 3.0, ((0, 16),)),
        "fc1_weight": scatter_about(seeds[12], (D, FF), D ** -0.5, 0.1875, ((0, 16),)),
        "fc1_bias": scatter_about(seeds[13], (FF,), 0.5, 3.0, ((0, 16),)),
        "fc2_weight": scatter_about(seeds[14], (FF, D), FF ** -0.5, 0.09375, ((0, 16),)),
        "fc2_bias": scatter_about(seeds[15], (D,), 0.5, 3.0, ((0, 16),)),
        "second_scale": jnp.clip(jnp.exp(math.log(2.0) - 1.3862944 * jax.random.uniform(seeds[16], (D,), jnp.float32) ** level_of(seeds[16], (D,), ((0, 16),), -0.2, 0.2)), 0.5, 2.0).astype(jnp.bfloat16),
        "cotangent": bell_draw_with(seeds[17], (IMAGES, LEN, D), 1.0, 6.0, ((0, 16), (1, 2)), (0, 2, 16, 2.0), jnp.float32),
    }


EPSILON = 1e-06
ROOT_HALF = 0.7071067811865476
INV_ROOT_TAU = 0.3989422804014327

def normalize(values, gain, shift):
    centre = values - lax.optimization_barrier(jnp.mean(values, axis=-1, keepdims=True))
    spread_inv = lax.rsqrt(lax.optimization_barrier(jnp.mean(centre * centre, axis=-1, keepdims=True)) + EPSILON)
    unit = centre * spread_inv
    return (unit * gain + shift, unit, spread_inv)

def normalize_back(grad_out, unit, spread_inv, gain):
    scaled = grad_out * gain
    return spread_inv * (scaled - lax.optimization_barrier(jnp.mean(scaled, axis=-1, keepdims=True)) - unit * lax.optimization_barrier(jnp.mean(scaled * unit, axis=-1, keepdims=True)))

def smooth_gate(values):
    return 0.5 * values * (1.0 + lax.erf(values * ROOT_HALF))

def gate_slope(values):
    return 0.5 * (1.0 + lax.erf(values * ROOT_HALF)) + values * jnp.exp(-0.5 * values * values) * INV_ROOT_TAU

def wide(values):
    return values.astype(jnp.float32)

def score_table(query, keys, valid):
    factor = query.shape[-1] ** (-0.5)
    scores = jnp.einsum('qhd,khd->hqk', wide(query), wide(keys)) * factor
    return jnp.where(valid[None, None, :], scores, -jnp.inf)

def attend(query, keys, values, valid):
    scores = score_table(query, keys, valid)
    row_top = lax.optimization_barrier(jnp.max(scores, axis=-1, keepdims=True))
    log_total = row_top + jnp.log(lax.optimization_barrier(jnp.sum(jnp.exp(scores - row_top), axis=-1, keepdims=True)))
    weights = jnp.exp(scores - log_total).astype(jnp.bfloat16)
    attended = jnp.einsum('hqk,khd->qhd', wide(weights), wide(values)).astype(jnp.bfloat16)
    return (attended, log_total)

def attend_back(query, keys, values, attended, log_total, grad_attended, valid):
    factor = query.shape[-1] ** (-0.5)
    scores = score_table(query, keys, valid)
    prob = jnp.exp(scores - log_total)
    weights = prob.astype(jnp.bfloat16)
    grad_values = jnp.einsum('hqk,qhd->khd', wide(weights), wide(grad_attended)).astype(jnp.bfloat16)
    grad_prob = jnp.einsum('qhd,khd->hqk', wide(grad_attended), wide(values))
    delta = jnp.einsum('qhd,qhd->hq', wide(grad_attended), wide(attended))[:, :, None]
    grad_scores = (prob * (grad_prob - delta) * factor).astype(jnp.bfloat16)
    grad_query = jnp.einsum('hqk,khd->qhd', wide(grad_scores), wide(keys)).astype(jnp.bfloat16)
    grad_keys = jnp.einsum('hqk,qhd->khd', wide(grad_scores), wide(query)).astype(jnp.bfloat16)
    return (grad_query, grad_keys, grad_values)

def reference(block_input, key_mask, first_gain, first_shift, qkv_weight, query_bias, value_bias, proj_weight, proj_bias, first_scale, second_gain, second_shift, fc1_weight, fc1_bias, fc2_weight, fc2_bias, second_scale, cotangent):
    joint_bias = jnp.concatenate([wide(query_bias), jnp.zeros((D,), jnp.float32), wide(value_bias)])
    params = (first_gain, first_shift, qkv_weight, query_bias, value_bias, proj_weight, proj_bias, first_scale, second_gain, second_shift, fc1_weight, fc1_bias, fc2_weight, fc2_bias, second_scale)
    zeros = tuple((jnp.zeros(item.shape, jnp.float32) for item in params))

    def one_image(totals, item):
        tokens, mask_row, grad_out = item
        valid = mask_row > 0
        normed1, unit1, inv1 = normalize(tokens, wide(first_gain), wide(first_shift))
        act1 = normed1.astype(jnp.bfloat16)
        joint = (jnp.dot(act1, qkv_weight, preferred_element_type=jnp.float32) + joint_bias).astype(jnp.bfloat16)
        query = joint[:, :D].reshape(LEN, HEADS, HD)
        keys = joint[:, D:2 * D].reshape(LEN, HEADS, HD)
        values = joint[:, 2 * D:].reshape(LEN, HEADS, HD)
        attended, log_total = attend(query, keys, values, valid)
        attended_flat = attended.reshape(LEN, D)
        mixed = jnp.dot(attended_flat, proj_weight, preferred_element_type=jnp.float32) + wide(proj_bias)
        resid = tokens + wide(first_scale) * mixed
        normed2, unit2, inv2 = normalize(resid, wide(second_gain), wide(second_shift))
        act2 = normed2.astype(jnp.bfloat16)
        pre = jnp.dot(act2, fc1_weight, preferred_element_type=jnp.float32) + wide(fc1_bias)
        hidden = smooth_gate(pre).astype(jnp.bfloat16)
        branch = jnp.dot(hidden, fc2_weight, preferred_element_type=jnp.float32) + wide(fc2_bias)
        result = resid + wide(second_scale) * branch
        grad_scale2 = lax.optimization_barrier(jnp.sum(grad_out * branch, axis=0))
        grad_branch = wide(second_scale) * grad_out
        grad_bias2 = lax.optimization_barrier(jnp.sum(grad_branch, axis=0))
        branch_low = grad_branch.astype(jnp.bfloat16)
        grad_fc2 = jnp.dot(hidden.T, branch_low, preferred_element_type=jnp.float32)
        grad_hidden = jnp.dot(branch_low, fc2_weight.T, preferred_element_type=jnp.float32)
        grad_pre = grad_hidden * gate_slope(pre)
        grad_bias1 = lax.optimization_barrier(jnp.sum(grad_pre, axis=0))
        pre_low = grad_pre.astype(jnp.bfloat16)
        grad_fc1 = jnp.dot(act2.T, pre_low, preferred_element_type=jnp.float32)
        grad_act2 = jnp.dot(pre_low, fc1_weight.T, preferred_element_type=jnp.float32)
        grad_gain2 = lax.optimization_barrier(jnp.sum(grad_act2 * unit2, axis=0))
        grad_shift2 = lax.optimization_barrier(jnp.sum(grad_act2, axis=0))
        grad_resid = grad_out + normalize_back(grad_act2, unit2, inv2, wide(second_gain))
        grad_scale1 = lax.optimization_barrier(jnp.sum(grad_resid * mixed, axis=0))
        grad_mixed = wide(first_scale) * grad_resid
        grad_pbias = lax.optimization_barrier(jnp.sum(grad_mixed, axis=0))
        mixed_low = grad_mixed.astype(jnp.bfloat16)
        grad_proj = jnp.dot(attended_flat.T, mixed_low, preferred_element_type=jnp.float32)
        grad_attended = jnp.dot(mixed_low, proj_weight.T, preferred_element_type=jnp.float32).astype(jnp.bfloat16)
        grad_query, grad_keys, grad_values = attend_back(query, keys, values, attended, log_total, grad_attended.reshape(LEN, HEADS, HD), valid)
        grad_joint = jnp.concatenate([grad_query.reshape(LEN, D), grad_keys.reshape(LEN, D), grad_values.reshape(LEN, D)], axis=1)
        grad_qbias = lax.optimization_barrier(jnp.sum(wide(grad_joint[:, :D]), axis=0))
        grad_vbias = lax.optimization_barrier(jnp.sum(wide(grad_joint[:, 2 * D:]), axis=0))
        grad_qkv = jnp.dot(act1.T, grad_joint, preferred_element_type=jnp.float32)
        grad_act1 = jnp.dot(grad_joint, qkv_weight.T, preferred_element_type=jnp.float32)
        grad_gain1 = lax.optimization_barrier(jnp.sum(grad_act1 * unit1, axis=0))
        grad_shift1 = lax.optimization_barrier(jnp.sum(grad_act1, axis=0))
        grad_in = grad_resid + normalize_back(grad_act1, unit1, inv1, wide(first_gain))
        terms = (grad_gain1, grad_shift1, grad_qkv, grad_qbias, grad_vbias, grad_proj, grad_pbias, grad_scale1, grad_gain2, grad_shift2, grad_fc1, grad_bias1, grad_fc2, grad_bias2, grad_scale2)
        totals = tuple((total + term for total, term in zip(totals, terms)))
        return (totals, (result, grad_in))
    totals, outputs = lax.scan(one_image, zeros, (block_input, key_mask, cotangent))
    return (outputs[0], outputs[1], totals[0], totals[1], totals[2], totals[3], totals[4], totals[5], totals[6], totals[7], totals[8], totals[9], totals[10], totals[11], totals[12], totals[13], totals[14])
```

```python
import jax
import jax.numpy as jnp
from jax import lax
from jax.sharding import PartitionSpec as P

HEADS = 16
HD = 64


EPSILON = 1e-06
ROOT_HALF = 0.7071067811865476
INV_ROOT_TAU = 0.3989422804014327


def normalize(values, gain, shift):
    centre = values - jnp.mean(values, axis=-1, keepdims=True)
    spread_inv = lax.rsqrt(jnp.mean(centre * centre, axis=-1, keepdims=True) + EPSILON)
    unit = centre * spread_inv
    return (unit * gain + shift, unit, spread_inv)


def normalize_back(grad_out, unit, spread_inv, gain):
    scaled = grad_out * gain
    return spread_inv * (
        scaled
        - jnp.mean(scaled, axis=-1, keepdims=True)
        - unit * jnp.mean(scaled * unit, axis=-1, keepdims=True)
    )


def smooth_gate(values):
    return 0.5 * values * (1.0 + lax.erf(values * ROOT_HALF))


def gate_slope(values):
    return (
        0.5 * (1.0 + lax.erf(values * ROOT_HALF))
        + values * jnp.exp(-0.5 * values * values) * INV_ROOT_TAU
    )


def wide(values):
    return values.astype(jnp.float32)


def score_table(query, keys, valid):
    factor = query.shape[-1] ** (-0.5)
    scores = jnp.einsum("qhd,khd->hqk", query, keys, preferred_element_type=jnp.float32) * factor
    return jnp.where(valid[None, None, :], scores, -jnp.inf)


def attend(query, keys, values, valid):
    scores = score_table(query, keys, valid)
    row_top = jnp.max(scores, axis=-1, keepdims=True)
    log_total = row_top + jnp.log(jnp.sum(jnp.exp(scores - row_top), axis=-1, keepdims=True))
    weights = jnp.exp(scores - log_total).astype(jnp.bfloat16)
    attended = jnp.einsum(
        "hqk,khd->qhd", weights, values, preferred_element_type=jnp.float32
    ).astype(jnp.bfloat16)
    return (attended, log_total)


def attend_back(query, keys, values, attended, log_total, grad_attended, valid):
    factor = query.shape[-1] ** (-0.5)
    scores = score_table(query, keys, valid)
    prob = jnp.exp(scores - log_total)
    weights = prob.astype(jnp.bfloat16)
    grad_values = jnp.einsum(
        "hqk,qhd->khd", weights, grad_attended, preferred_element_type=jnp.float32
    ).astype(jnp.bfloat16)
    grad_prob = jnp.einsum(
        "qhd,khd->hqk", grad_attended, values, preferred_element_type=jnp.float32
    )
    delta = jnp.einsum("qhd,qhd->hq", grad_attended, attended, preferred_element_type=jnp.float32)[
        :, :, None
    ]
    grad_scores = (prob * (grad_prob - delta) * factor).astype(jnp.bfloat16)
    grad_query = jnp.einsum(
        "hqk,khd->qhd", grad_scores, keys, preferred_element_type=jnp.float32
    ).astype(jnp.bfloat16)
    grad_keys = jnp.einsum(
        "hqk,qhd->khd", grad_scores, query, preferred_element_type=jnp.float32
    ).astype(jnp.bfloat16)
    return (grad_query, grad_keys, grad_values)


def level_pairs(bit):
    count = lax.axis_size("fsdp")
    return [(i, i ^ (1 << bit)) for i in range(count)]


def my_bit(bit):
    return (lax.axis_index("fsdp") >> bit) & 1


def levels():
    return int(lax.axis_size("fsdp")).bit_length() - 1


def gather_by_doubling(block):
    shape = block.shape
    held, done = block, []
    for bit in list(range(2, levels())) + [1, 0]:
        other = lax.ppermute(held, "fsdp", level_pairs(bit))
        mine_first = my_bit(bit) == 0
        place = sum(1 for earlier in done if earlier > bit)
        held = jnp.stack(
            [jnp.where(mine_first, held, other), jnp.where(mine_first, other, held)], axis=place
        )
        done.append(bit)
    return held.reshape((-1,) + shape[1:])


def scatter_by_halving(terms):
    count, top = lax.axis_size("fsdp"), levels()
    rows = terms.shape[0] // count
    held = terms.reshape((2,) * top + (rows,) + terms.shape[1:])
    left = list(range(top))[::-1]
    total = None
    for bit in [0, 1] + list(range(2, top))[::-1]:
        place = left.index(bit)
        mine = my_bit(bit)
        sent = lax.dynamic_index_in_dim(held, 1 - mine, place, keepdims=False)
        kept = lax.dynamic_index_in_dim(held, mine, place, keepdims=False)
        other = lax.ppermute(sent, "fsdp", level_pairs(bit))
        total = wide(kept) + wide(other)
        held = total.astype(jnp.bfloat16)
        left.remove(bit)
    return held


def owned_rows(terms, by_halving):
    if by_halving:
        part = scatter_by_halving(terms)
    else:
        part = lax.psum_scatter(terms, "fsdp", scatter_dimension=0, tiled=True)
    count = lax.axis_size("seq")
    total = wide(part)
    for step in range(1, count):
        other = lax.ppermute(part, "seq", [(i, (i + step) % count) for i in range(count)])
        total = total + wide(other)
    return total


def on_device(
    block_input,
    key_mask,
    first_gain,
    first_shift,
    qkv_weight,
    query_bias,
    value_bias,
    proj_weight,
    proj_bias,
    first_scale,
    second_gain,
    second_shift,
    fc1_weight,
    fc1_bias,
    fc2_weight,
    fc2_bias,
    second_scale,
    cotangent,
):
    rows = first_gain.shape[0]
    vectors = (
        first_gain,
        first_shift,
        query_bias,
        value_bias,
        proj_bias,
        first_scale,
        second_gain,
        second_shift,
        fc2_bias,
        second_scale,
    )
    ratio = fc1_bias.shape[0] // rows
    columns = jnp.concatenate(
        [jnp.stack(vectors, axis=1), fc1_bias.reshape(rows, ratio)], axis=1
    )
    spare = 128 - columns.shape[1]
    columns = jnp.pad(columns, ((0, 0), (0, spare)))
    joint_all = lax.all_gather(
        jnp.concatenate([qkv_weight, columns], axis=1), "fsdp", axis=0, tiled=True
    )
    proj_full = lax.all_gather(proj_weight, "fsdp", axis=0, tiled=True)
    expand_full = lax.all_gather(fc1_weight, "fsdp", axis=0, tiled=True)
    reduce_full = gather_by_doubling(fc2_weight)
    joint_cols = qkv_weight.shape[1]
    joint_full = joint_all[:, :joint_cols]
    small = joint_all[:, joint_cols:]
    small_t = small.T
    (
        gain_one,
        shift_one,
        qbias_full,
        vbias_full,
        pbias_full,
        scale_one,
        gain_two,
        shift_two,
        rbias_full,
        scale_two,
    ) = tuple(small_t[i] for i in range(10))
    ebias_full = small[:, 10 : 10 + ratio].reshape(-1)
    width = joint_full.shape[0]
    tokens = block_input[0]
    count = tokens.shape[0]
    valid = key_mask[0] > 0
    length = valid.shape[0]
    seq_count = lax.axis_size("seq")
    heads_here = HEADS // seq_count
    local_cols = heads_here * HD
    normed1, unit1, inv1 = normalize(tokens, wide(gain_one), wide(shift_one))
    act1 = normed1.astype(jnp.bfloat16)
    joint_bias = jnp.concatenate(
        [wide(qbias_full), jnp.zeros((width,), jnp.float32), wide(vbias_full)]
    )
    joint = (jnp.dot(act1, joint_full, preferred_element_type=jnp.float32) + joint_bias).astype(
        jnp.bfloat16
    )
    spread = lax.all_to_all(
        joint.reshape(count, 3, seq_count, local_cols),
        "seq",
        split_axis=2,
        concat_axis=0,
        tiled=True,
    )
    spread = spread.reshape(length, 3, heads_here, HD)
    query = spread[:, 0]
    keys = spread[:, 1]
    values = spread[:, 2]
    attended, log_total = attend(query, keys, values, valid)
    returned = lax.all_to_all(
        attended.reshape(length, 1, local_cols), "seq", split_axis=0, concat_axis=1, tiled=True
    )
    attended_flat = returned.reshape(count, width)
    mixed = jnp.dot(attended_flat, proj_full, preferred_element_type=jnp.float32) + wide(pbias_full)
    resid = tokens + wide(scale_one) * mixed
    normed2, unit2, inv2 = normalize(resid, wide(gain_two), wide(shift_two))
    act2 = normed2.astype(jnp.bfloat16)
    pre = jnp.dot(act2, expand_full, preferred_element_type=jnp.float32) + wide(ebias_full)
    hidden = smooth_gate(pre).astype(jnp.bfloat16)
    branch = jnp.dot(hidden, reduce_full, preferred_element_type=jnp.float32) + wide(rbias_full)
    result = resid + wide(scale_two) * branch
    grad_out = cotangent[0]
    grad_scale2 = jnp.sum(grad_out * branch, axis=0)
    grad_branch = wide(scale_two) * grad_out
    grad_bias2 = jnp.sum(grad_branch, axis=0)
    branch_low = grad_branch.astype(jnp.bfloat16)
    grad_reduce = jnp.einsum("tf,td->fd", hidden, branch_low, preferred_element_type=jnp.float32)
    reduce_low = grad_reduce.astype(jnp.bfloat16)
    reduce_low, branch_low = lax.optimization_barrier((reduce_low, branch_low))
    own_fc2 = owned_rows(reduce_low, True)
    grad_hidden = jnp.einsum(
        "td,fd->tf", branch_low, reduce_full, preferred_element_type=jnp.float32
    )
    grad_pre = grad_hidden * gate_slope(pre)
    grad_bias1 = jnp.sum(grad_pre, axis=0)
    pre_low = grad_pre.astype(jnp.bfloat16)
    grad_expand = jnp.einsum("td,tf->df", act2, pre_low, preferred_element_type=jnp.float32)
    expand_low = grad_expand.astype(jnp.bfloat16)
    expand_low, pre_low = lax.optimization_barrier((expand_low, pre_low))
    own_fc1 = owned_rows(expand_low, False)
    grad_act2 = jnp.einsum("tf,df->td", pre_low, expand_full, preferred_element_type=jnp.float32)
    grad_gain2 = jnp.sum(grad_act2 * unit2, axis=0)
    grad_shift2 = jnp.sum(grad_act2, axis=0)
    grad_resid = grad_out + normalize_back(grad_act2, unit2, inv2, wide(gain_two))
    grad_scale1 = jnp.sum(grad_resid * mixed, axis=0)
    grad_mixed = wide(scale_one) * grad_resid
    grad_pbias = jnp.sum(grad_mixed, axis=0)
    mixed_low = grad_mixed.astype(jnp.bfloat16)
    grad_proj = jnp.einsum(
        "td,te->de", attended_flat, mixed_low, preferred_element_type=jnp.float32
    )
    proj_low = grad_proj.astype(jnp.bfloat16)
    proj_low, mixed_low = lax.optimization_barrier((proj_low, mixed_low))
    own_proj = owned_rows(proj_low, False)
    grad_attended = jnp.einsum(
        "te,de->td", mixed_low, proj_full, preferred_element_type=jnp.float32
    ).astype(jnp.bfloat16)
    grad_spread = lax.all_to_all(
        grad_attended.reshape(count, seq_count, local_cols),
        "seq",
        split_axis=1,
        concat_axis=0,
        tiled=True,
    )
    grad_heads = grad_spread.reshape(length, heads_here, HD)
    grad_query, grad_keys, grad_values = attend_back(
        query, keys, values, attended, log_total, grad_heads, valid
    )
    stacked = jnp.stack((grad_query, grad_keys, grad_values), axis=1).reshape(
        length, 3, 1, local_cols
    )
    grad_back = lax.all_to_all(stacked, "seq", split_axis=0, concat_axis=2, tiled=True)
    grad_joint = grad_back.reshape(count, 3 * width)
    grad_qbias = jnp.sum(wide(grad_joint[:, :width]), axis=0)
    grad_vbias = jnp.sum(wide(grad_joint[:, 2 * width :]), axis=0)
    grad_qkv = jnp.einsum("td,te->de", act1, grad_joint, preferred_element_type=jnp.float32)
    grad_act1 = jnp.einsum("te,de->td", grad_joint, joint_full, preferred_element_type=jnp.float32)
    grad_gain1 = jnp.sum(grad_act1 * unit1, axis=0)
    grad_shift1 = jnp.sum(grad_act1, axis=0)
    grad_in = grad_resid + normalize_back(grad_act1, unit1, inv1, wide(gain_one))
    sums = jnp.stack(
        (
            grad_gain1,
            grad_shift1,
            grad_qbias,
            grad_vbias,
            grad_pbias,
            grad_scale1,
            grad_gain2,
            grad_shift2,
            grad_bias2,
            grad_scale2,
        ),
        axis=1,
    )
    sums = jnp.concatenate([sums, grad_bias1.reshape(width, ratio)], axis=1)
    sums = jnp.pad(sums, ((0, 0), (0, spare)))
    last = jnp.concatenate([grad_qkv.astype(jnp.bfloat16), sums.astype(jnp.bfloat16)], axis=1)
    own_last = owned_rows(last, True)
    own_qkv = own_last[:, :joint_cols]
    own_small = own_last[:, joint_cols:].T
    (
        own_g1,
        own_s1,
        own_qb,
        own_vb,
        own_pb,
        own_l1,
        own_g2,
        own_s2,
        own_b2,
        own_l2,
    ) = tuple(own_small[i] for i in range(10))
    own_b1 = own_last[:, joint_cols + 10 : joint_cols + 10 + ratio].reshape(-1)
    summed = (
        own_g1,
        own_s1,
        own_qkv,
        own_qb,
        own_vb,
        own_proj,
        own_pb,
        own_l1,
        own_g2,
        own_s2,
        own_fc1,
        own_b1,
        own_fc2,
        own_b2,
        own_l2,
    )
    return (
        result[None],
        grad_in[None],
        summed[0],
        summed[1],
        summed[2],
        summed[3],
        summed[4],
        summed[5],
        summed[6],
        summed[7],
        summed[8],
        summed[9],
        summed[10],
        summed[11],
        summed[12],
        summed[13],
        summed[14],
    )


def solution(mesh):
    return jax.shard_map(
        on_device,
        mesh=mesh,
        in_specs=(
            P("fsdp", "seq", None),
            P("fsdp", None),
            P("fsdp"),
            P("fsdp"),
            P("fsdp", None),
            P("fsdp"),
            P("fsdp"),
            P("fsdp", None),
            P("fsdp"),
            P("fsdp"),
            P("fsdp"),
            P("fsdp"),
            P("fsdp", None),
            P("fsdp"),
            P("fsdp", None),
            P("fsdp"),
            P("fsdp"),
            P("fsdp", "seq", None),
        ),
        out_specs=(
            P("fsdp", "seq", None),
            P("fsdp", "seq", None),
            P("fsdp"),
            P("fsdp"),
            P("fsdp", None),
            P("fsdp"),
            P("fsdp"),
            P("fsdp", None),
            P("fsdp"),
            P("fsdp"),
            P("fsdp"),
            P("fsdp"),
            P("fsdp", None),
            P("fsdp"),
            P("fsdp", None),
            P("fsdp"),
            P("fsdp"),
        ),
        check_vma=False,
    )
```

```python
import jax
import jax.numpy as jnp
from jax import lax
from jax.sharding import PartitionSpec as P

HEADS = 16
HD = 64


EPSILON = 1e-06
ROOT_HALF = 0.7071067811865476
INV_ROOT_TAU = 0.3989422804014327


def normalize(values, gain, shift):
    centre = values - jnp.mean(values, axis=-1, keepdims=True)
    spread_inv = lax.rsqrt(jnp.mean(centre * centre, axis=-1, keepdims=True) + EPSILON)
    unit = centre * spread_inv
    return (unit * gain + shift, unit, spread_inv)


def normalize_back(grad_out, unit, spread_inv, gain):
    scaled = grad_out * gain
    return spread_inv * (
        scaled
        - jnp.mean(scaled, axis=-1, keepdims=True)
        - unit * jnp.mean(scaled * unit, axis=-1, keepdims=True)
    )


def smooth_gate(values):
    return 0.5 * values * (1.0 + lax.erf(values * ROOT_HALF))


def gate_slope(values):
    return (
        0.5 * (1.0 + lax.erf(values * ROOT_HALF))
        + values * jnp.exp(-0.5 * values * values) * INV_ROOT_TAU
    )


def wide(values):
    return values.astype(jnp.float32)


def score_table(query, keys, valid):
    factor = query.shape[-1] ** (-0.5)
    scores = jnp.einsum("qhd,khd->hqk", query, keys, preferred_element_type=jnp.float32) * factor
    return jnp.where(valid[None, None, :], scores, -jnp.inf)


def attend(query, keys, values, valid):
    scores = score_table(query, keys, valid)
    row_top = jnp.max(scores, axis=-1, keepdims=True)
    log_total = row_top + jnp.log(jnp.sum(jnp.exp(scores - row_top), axis=-1, keepdims=True))
    weights = jnp.exp(scores - log_total).astype(jnp.bfloat16)
    attended = jnp.einsum(
        "hqk,khd->qhd", weights, values, preferred_element_type=jnp.float32
    ).astype(jnp.bfloat16)
    return (attended, log_total)


def attend_back(query, keys, values, attended, log_total, grad_attended, valid):
    factor = query.shape[-1] ** (-0.5)
    scores = score_table(query, keys, valid)
    prob = jnp.exp(scores - log_total)
    weights = prob.astype(jnp.bfloat16)
    grad_values = jnp.einsum(
        "hqk,qhd->khd", weights, grad_attended, preferred_element_type=jnp.float32
    ).astype(jnp.bfloat16)
    grad_prob = jnp.einsum(
        "qhd,khd->hqk", grad_attended, values, preferred_element_type=jnp.float32
    )
    delta = jnp.einsum("qhd,qhd->hq", grad_attended, attended, preferred_element_type=jnp.float32)[
        :, :, None
    ]
    grad_scores = (prob * (grad_prob - delta) * factor).astype(jnp.bfloat16)
    grad_query = jnp.einsum(
        "hqk,khd->qhd", grad_scores, keys, preferred_element_type=jnp.float32
    ).astype(jnp.bfloat16)
    grad_keys = jnp.einsum(
        "hqk,qhd->khd", grad_scores, query, preferred_element_type=jnp.float32
    ).astype(jnp.bfloat16)
    return (grad_query, grad_keys, grad_values)


def level_pairs(bit):
    count = lax.axis_size("fsdp")
    return [(i, i ^ (1 << bit)) for i in range(count)]


def my_bit(bit):
    return (lax.axis_index("fsdp") >> bit) & 1


def levels():
    return int(lax.axis_size("fsdp")).bit_length() - 1


def gather_by_doubling(block):
    shape = block.shape
    held, done = block, []
    for bit in list(range(2, levels())) + [1, 0]:
        other = lax.ppermute(held, "fsdp", level_pairs(bit))
        mine_first = my_bit(bit) == 0
        place = sum(1 for earlier in done if earlier > bit)
        held = jnp.stack(
            [jnp.where(mine_first, held, other), jnp.where(mine_first, other, held)], axis=place
        )
        done.append(bit)
    return held.reshape((-1,) + shape[1:])


def scatter_by_halving(terms):
    count, top = lax.axis_size("fsdp"), levels()
    rows = terms.shape[0] // count
    held = terms.reshape((2,) * top + (rows,) + terms.shape[1:])
    left = list(range(top))[::-1]
    total = None
    for bit in [0, 1] + list(range(2, top))[::-1]:
        place = left.index(bit)
        mine = my_bit(bit)
        sent = lax.dynamic_index_in_dim(held, 1 - mine, place, keepdims=False)
        kept = lax.dynamic_index_in_dim(held, mine, place, keepdims=False)
        other = lax.ppermute(sent, "fsdp", level_pairs(bit))
        total = wide(kept) + wide(other)
        held = total.astype(jnp.bfloat16)
        left.remove(bit)
    return held


def after(values, earlier):
    spot = earlier[(0,) * earlier.ndim]
    return values + jnp.minimum(jnp.abs(spot), 0).astype(values.dtype)


def owned_rows(terms, by_halving):
    if by_halving:
        part = scatter_by_halving(terms)
    else:
        part = lax.psum_scatter(terms, "fsdp", scatter_dimension=0, tiled=True)
    count = lax.axis_size("seq")
    total = wide(part)
    for step in range(1, count):
        other = lax.ppermute(part, "seq", [(i, (i + step) % count) for i in range(count)])
        total = total + wide(other)
    return total


def on_device(
    block_input,
    key_mask,
    first_gain,
    first_shift,
    qkv_weight,
    query_bias,
    value_bias,
    proj_weight,
    proj_bias,
    first_scale,
    second_gain,
    second_shift,
    fc1_weight,
    fc1_bias,
    fc2_weight,
    fc2_bias,
    second_scale,
    cotangent,
):
    rows = first_gain.shape[0]
    vectors = (
        first_gain,
        first_shift,
        query_bias,
        value_bias,
        proj_bias,
        first_scale,
        second_gain,
        second_shift,
        fc2_bias,
        second_scale,
    )
    ratio = fc1_bias.shape[0] // rows
    columns = jnp.concatenate(
        [jnp.stack(vectors, axis=1), fc1_bias.reshape(rows, ratio)], axis=1
    )
    spare = 128 - columns.shape[1]
    columns = jnp.pad(columns, ((0, 0), (0, spare)))
    joint_all = lax.all_gather(
        jnp.concatenate([qkv_weight, columns], axis=1), "fsdp", axis=0, tiled=True
    )
    proj_full = lax.all_gather(proj_weight, "fsdp", axis=0, tiled=True)
    expand_full = lax.all_gather(fc1_weight, "fsdp", axis=0, tiled=True)
    reduce_full = gather_by_doubling(fc2_weight)
    joint_cols = qkv_weight.shape[1]
    joint_full = joint_all[:, :joint_cols]
    small = joint_all[:, joint_cols:]
    small_t = small.T
    (
        gain_one,
        shift_one,
        qbias_full,
        vbias_full,
        pbias_full,
        scale_one,
        gain_two,
        shift_two,
        rbias_full,
        scale_two,
    ) = tuple(small_t[i] for i in range(10))
    ebias_full = small[:, 10 : 10 + ratio].reshape(-1)
    width = joint_full.shape[0]
    tokens = block_input[0]
    count = tokens.shape[0]
    valid = key_mask[0] > 0
    length = valid.shape[0]
    seq_count = lax.axis_size("seq")
    heads_here = HEADS // seq_count
    local_cols = heads_here * HD
    normed1, unit1, inv1 = normalize(tokens, wide(gain_one), wide(shift_one))
    act1 = normed1.astype(jnp.bfloat16)
    joint_bias = jnp.concatenate(
        [wide(qbias_full), jnp.zeros((width,), jnp.float32), wide(vbias_full)]
    )
    joint = (jnp.dot(act1, joint_full, preferred_element_type=jnp.float32) + joint_bias).astype(
        jnp.bfloat16
    )
    spread = lax.all_to_all(
        joint.reshape(count, 3, seq_count, local_cols),
        "seq",
        split_axis=2,
        concat_axis=0,
        tiled=True,
    )
    spread = spread.reshape(length, 3, heads_here, HD)
    query = spread[:, 0]
    keys = spread[:, 1]
    values = spread[:, 2]
    attended, log_total = attend(query, keys, values, valid)
    returned = lax.all_to_all(
        attended.reshape(length, 1, local_cols), "seq", split_axis=0, concat_axis=1, tiled=True
    )
    attended_flat = returned.reshape(count, width)
    mixed = jnp.dot(attended_flat, proj_full, preferred_element_type=jnp.float32) + wide(pbias_full)
    resid = tokens + wide(scale_one) * mixed
    normed2, unit2, inv2 = normalize(resid, wide(gain_two), wide(shift_two))
    act2 = normed2.astype(jnp.bfloat16)
    pre = jnp.dot(act2, expand_full, preferred_element_type=jnp.float32) + wide(ebias_full)
    hidden = smooth_gate(pre).astype(jnp.bfloat16)
    branch = jnp.dot(hidden, reduce_full, preferred_element_type=jnp.float32) + wide(rbias_full)
    result = resid + wide(scale_two) * branch
    grad_out = cotangent[0]
    grad_scale2 = jnp.sum(grad_out * branch, axis=0)
    grad_branch = wide(scale_two) * grad_out
    grad_bias2 = jnp.sum(grad_branch, axis=0)
    branch_low = grad_branch.astype(jnp.bfloat16)
    grad_reduce = jnp.einsum("tf,td->fd", hidden, branch_low, preferred_element_type=jnp.float32)
    reduce_low = grad_reduce.astype(jnp.bfloat16)
    reduce_low, branch_low = lax.optimization_barrier((reduce_low, branch_low))
    own_fc2 = owned_rows(reduce_low, True)
    grad_hidden = jnp.einsum(
        "td,fd->tf", branch_low, reduce_full, preferred_element_type=jnp.float32
    )
    grad_pre = grad_hidden * gate_slope(pre)
    grad_bias1 = jnp.sum(grad_pre, axis=0)
    pre_low = grad_pre.astype(jnp.bfloat16)
    grad_expand = jnp.einsum("td,tf->df", act2, pre_low, preferred_element_type=jnp.float32)
    expand_low = grad_expand.astype(jnp.bfloat16)
    expand_low, pre_low = lax.optimization_barrier((expand_low, pre_low))
    own_fc1 = owned_rows(expand_low, False)
    grad_act2 = jnp.einsum("tf,df->td", pre_low, expand_full, preferred_element_type=jnp.float32)
    grad_gain2 = jnp.sum(grad_act2 * unit2, axis=0)
    grad_shift2 = jnp.sum(grad_act2, axis=0)
    grad_resid = grad_out + normalize_back(grad_act2, unit2, inv2, wide(gain_two))
    grad_scale1 = jnp.sum(grad_resid * mixed, axis=0)
    grad_mixed = wide(scale_one) * grad_resid
    grad_pbias = jnp.sum(grad_mixed, axis=0)
    mixed_low = grad_mixed.astype(jnp.bfloat16)
    grad_proj = jnp.einsum(
        "td,te->de", attended_flat, mixed_low, preferred_element_type=jnp.float32
    )
    proj_low = grad_proj.astype(jnp.bfloat16)
    proj_low = after(proj_low, own_fc1)
    own_proj = owned_rows(proj_low, False)
    grad_attended = jnp.einsum(
        "te,de->td", mixed_low, proj_full, preferred_element_type=jnp.float32
    ).astype(jnp.bfloat16)
    grad_spread = lax.all_to_all(
        grad_attended.reshape(count, seq_count, local_cols),
        "seq",
        split_axis=1,
        concat_axis=0,
        tiled=True,
    )
    grad_heads = grad_spread.reshape(length, heads_here, HD)
    grad_query, grad_keys, grad_values = attend_back(
        query, keys, values, attended, log_total, grad_heads, valid
    )
    stacked = jnp.stack((grad_query, grad_keys, grad_values), axis=1).reshape(
        length, 3, 1, local_cols
    )
    grad_back = lax.all_to_all(stacked, "seq", split_axis=0, concat_axis=2, tiled=True)
    grad_joint = grad_back.reshape(count, 3 * width)
    grad_qbias = jnp.sum(wide(grad_joint[:, :width]), axis=0)
    grad_vbias = jnp.sum(wide(grad_joint[:, 2 * width :]), axis=0)
    grad_qkv = jnp.einsum("td,te->de", act1, grad_joint, preferred_element_type=jnp.float32)
    grad_act1 = jnp.einsum("te,de->td", grad_joint, joint_full, preferred_element_type=jnp.float32)
    grad_gain1 = jnp.sum(grad_act1 * unit1, axis=0)
    grad_shift1 = jnp.sum(grad_act1, axis=0)
    grad_in = grad_resid + normalize_back(grad_act1, unit1, inv1, wide(gain_one))
    sums = jnp.stack(
        (
            grad_gain1,
            grad_shift1,
            grad_qbias,
            grad_vbias,
            grad_pbias,
            grad_scale1,
            grad_gain2,
            grad_shift2,
            grad_bias2,
            grad_scale2,
        ),
        axis=1,
    )
    sums = jnp.concatenate([sums, grad_bias1.reshape(width, ratio)], axis=1)
    sums = jnp.pad(sums, ((0, 0), (0, spare)))
    last = jnp.concatenate([grad_qkv.astype(jnp.bfloat16), sums.astype(jnp.bfloat16)], axis=1)
    own_last = owned_rows(last, True)
    own_qkv = own_last[:, :joint_cols]
    own_small = own_last[:, joint_cols:].T
    (
        own_g1,
        own_s1,
        own_qb,
        own_vb,
        own_pb,
        own_l1,
        own_g2,
        own_s2,
        own_b2,
        own_l2,
    ) = tuple(own_small[i] for i in range(10))
    own_b1 = own_last[:, joint_cols + 10 : joint_cols + 10 + ratio].reshape(-1)
    summed = (
        own_g1,
        own_s1,
        own_qkv,
        own_qb,
        own_vb,
        own_proj,
        own_pb,
        own_l1,
        own_g2,
        own_s2,
        own_fc1,
        own_b1,
        own_fc2,
        own_b2,
        own_l2,
    )
    return (
        result[None],
        grad_in[None],
        summed[0],
        summed[1],
        summed[2],
        summed[3],
        summed[4],
        summed[5],
        summed[6],
        summed[7],
        summed[8],
        summed[9],
        summed[10],
        summed[11],
        summed[12],
        summed[13],
        summed[14],
    )


def solution(mesh):
    return jax.shard_map(
        on_device,
        mesh=mesh,
        in_specs=(
            P("fsdp", "seq", None),
            P("fsdp", None),
            P("fsdp"),
            P("fsdp"),
            P("fsdp", None),
            P("fsdp"),
            P("fsdp"),
            P("fsdp", None),
            P("fsdp"),
            P("fsdp"),
            P("fsdp"),
            P("fsdp"),
            P("fsdp", None),
            P("fsdp"),
            P("fsdp", None),
            P("fsdp"),
            P("fsdp"),
            P("fsdp", "seq", None),
        ),
        out_specs=(
            P("fsdp", "seq", None),
            P("fsdp", "seq", None),
            P("fsdp"),
            P("fsdp"),
            P("fsdp", None),
            P("fsdp"),
            P("fsdp"),
            P("fsdp", None),
            P("fsdp"),
            P("fsdp"),
            P("fsdp"),
            P("fsdp"),
            P("fsdp", None),
            P("fsdp"),
            P("fsdp", None),
            P("fsdp"),
            P("fsdp"),
        ),
        check_vma=False,
    )
```
